32 devices in a mesh: grp: 4 (over x, core), dev: 8 (over z, y).
Axes of the slice: x: 2, y: 2, z: 4, core: 2. Of those that a mesh axis runs over, the one named last changes fastest.
Arguments:
- right_side: float32 [3072, 512], P(('grp', 'dev')), may hold values from -6 to 6
- ghost_rows: int32 [64, 24], P(('grp', 'dev')), may hold values from 0 to 95
- cols_one: int32 [3072, 2], P(('grp', 'dev')), may hold values from 0 to 143
- diag_one: float32 [3072, 4096], P(('grp', 'dev')), may hold values from -1 to 7
- offd_one: float32 [3072, 2, 4096], P(('grp', 'dev')), may hold values from -0.75 to 0.75
- prol_one: float32 [3072, 4096], P(('grp', 'dev')), may hold values from -0.75 to 0.75
- agg_one: int32 [3072], P(('grp', 'dev')), may hold values from 0 to 95
- cols_two: int32 [1536, 2], P(('grp', 'dev')), may hold values from 0 to 287, as said below
- diag_two: float32 [1536, 4096], P(('grp', 'dev')), may hold values from -1 to 7
- offd_two: float32 [1536, 2, 4096], P(('grp', 'dev')), may hold values from -0.75 to 0.75
- prol_two: float32 [1536, 4096], P(('grp', 'dev')), may hold values from -0.375 to 0.375
- agg_two: int32 [1536], P(('grp', 'dev')), may hold values from 0 to 31
- cols_three: int32 [32, 2], replicated, may hold values from 0 to 31
- diag_three: float32 [32, 4096], replicated, may hold values from -1 to 7
- offd_three: float32 [32, 2, 4096], replicated, may hold values from -0.75 to 0.75
Outputs:
- solution: float32 [3072, 512], P(('grp', 'dev'))
- coarse_solution: float32 [32, 512], replicated
The draws below stay inside these ranges and needn't reach their ends.
Inputs may be any that keep to these rules, and one draw needn't show every extreme that they name: `cols_two`: columns k = 0, 2, 4, ... read only pair blocks p - 1 and p (values below 192); columns k = 1, 3, 5, ... read only pair blocks p and p + 1 (values from 96 on).
All inputs are finite; a program needn't handle non-finite values.
Results may differ from the reference program's by a relative error of at most 0.00011.
Values sent between devices are 32-bit elements; how exact they have to be, the bound alone decides.
A program may use at most 128 MiB of HBM per device.

```python
import jax
import jax.numpy as jnp
from jax import lax

TILE = 64
LOADS = 8
ROWS = 96
OFFD = 2
COARSE = 32
DEGREE = 3
COARSE_DEGREE = 8
GHOST = 24
BLOCKS = 32
PAIRS = 16
ROWS_ALL = 3072
HALF_ALL = 1536


def dominant_tiles(key, row_count):
    flat_index = jnp.arange(TILE * TILE)
    on_diagonal = (flat_index % (TILE + 1) == 0).astype(jnp.float32)
    scale_key, dense_key = jax.random.split(key)
    diag_level = jax.random.uniform(scale_key, (row_count, 1), jnp.float32, 3.2, 6.4)
    dense_part = jnp.clip(jax.random.normal(dense_key, (row_count, TILE * TILE), jnp.float32), -4.0, 4.0)
    return diag_level * on_diagonal + dense_part * (0.35 / TILE ** 0.5)


def draw_diag_one(key, part):
    return dominant_tiles(jax.random.fold_in(key, 11), ROWS_ALL)


def draw_diag_two(key, part):
    return dominant_tiles(jax.random.fold_in(key, 23), HALF_ALL)


def draw_diag_three(key, part):
    return dominant_tiles(jax.random.fold_in(key, 37), COARSE)


def draw_cols_two(key, part):
    offsets = jax.random.randint(jax.random.fold_in(key, 41), (HALF_ALL, OFFD), 0, 2 * ROWS, jnp.int32)
    sides = jnp.arange(OFFD, dtype=jnp.int32) % 2 * ROWS
    return offsets + sides[None, :]


def plant(values, stream_key, smallest, high):
    shape = values.shape
    index_at = [jax.random.randint(jax.random.fold_in(stream_key, axis), (), 0, shape[axis]) for axis in range(len(shape))]
    values = values.at[tuple(index_at)].set(smallest)
    longest = shape.index(max(shape))
    index_at[longest] = (index_at[longest] + 1) % shape[longest]
    return values.at[tuple(index_at)].set(high)


def steps_of(own_key, dims, pieces, least, top_value):
    level, own = 1.0, jax.random.fold_in(own_key, 6)
    for dim, blocks in pieces:
        draws = jnp.exp(jax.random.uniform(jax.random.fold_in(own, dim), (blocks,), jnp.float32, least / len(pieces), top_value / len(pieces)))
        level = level * jnp.repeat(draws, dims[dim] // blocks).reshape([-1 if axis == dim else 1 for axis in range(len(dims))])
    return level


def gaussian(key, shape, deviation, reach, shards=(), kind=jnp.bfloat16):
    values = deviation * jax.random.normal(key, shape, jnp.float32)
    if shards:
        values = values * steps_of(key, shape, shards, -0.22, 0.18)
    return jnp.clip(values, -reach, reach).astype(kind)


def setup_inputs(seed: int = 0) -> dict:
    seeds = jax.random.split(jax.random.key(seed), 16)
    right_side = gaussian(seeds[0], (ROWS_ALL, LOADS * TILE), 1.0, 6.0, ((0, 32),), jnp.float32)
    ghost_rows = plant(jax.random.randint(seeds[1], (2 * BLOCKS, GHOST), 0, ROWS), jax.random.fold_in(seeds[1], 1), 0, ROWS - 1).astype(jnp.int32)
    cols_one = plant(jax.random.randint(seeds[2], (ROWS_ALL, OFFD), 0, ROWS + 2 * GHOST), jax.random.fold_in(seeds[2], 1), 0, (ROWS + 2 * GHOST) - 1).astype(jnp.int32)
    diag_one = draw_diag_one(jax.random.fold_in(seeds[15], 71), 0)
    offd_one = gaussian(seeds[4], (ROWS_ALL, OFFD, TILE * TILE), TILE ** -0.5, 0.75, ((0, 32),), jnp.float32)
    prol_one = gaussian(seeds[5], (ROWS_ALL, TILE * TILE), TILE ** -0.5, 0.75, ((0, 32),), jnp.float32)
    agg_one = plant(jax.random.randint(seeds[6], (ROWS_ALL,), 0, ROWS), jax.random.fold_in(seeds[6], 1), 0, ROWS - 1).astype(jnp.int32)
    cols_two = draw_cols_two(jax.random.fold_in(seeds[15], 71), 0)
    diag_two = draw_diag_two(jax.random.fold_in(seeds[15], 71), 0)
    offd_two = gaussian(seeds[9], (HALF_ALL, OFFD, TILE * TILE), TILE ** -0.5, 0.75, ((0, 32),), jnp.float32)
    prol_two = gaussian(seeds[10], (HALF_ALL, TILE * TILE), (4 * TILE) ** -0.5, 0.375, ((0, 32),), jnp.float32)
    agg_two = plant(jax.random.randint(seeds[11], (HALF_ALL,), 0, COARSE), jax.random.fold_in(seeds[11], 1), 0, COARSE - 1).astype(jnp.int32)
    cols_three = plant(jax.random.randint(seeds[12], (COARSE, OFFD), 0, COARSE), jax.random.fold_in(seeds[12], 1), 0, COARSE - 1).astype(jnp.int32)
    diag_three = draw_diag_three(jax.random.fold_in(seeds[15], 71), 0)
    offd_three = gaussian(seeds[14], (COARSE, OFFD, TILE * TILE), TILE ** -0.5, 0.75, (), jnp.float32)
    return {"right_side": right_side, "ghost_rows": ghost_rows, "cols_one": cols_one, "diag_one": diag_one, "offd_one": offd_one, "prol_one": prol_one, "agg_one": agg_one, "cols_two": cols_two, "diag_two": diag_two, "offd_two": offd_two, "prol_two": prol_two, "agg_two": agg_two, "cols_three": cols_three, "diag_three": diag_three, "offd_three": offd_three}


cheb_low = 1.0
cheb_high = 9.0
highest = lax.Precision.HIGHEST


def as_tiles(flat_tile):
    return flat_tile.reshape(flat_tile.shape[:-1] + (TILE, TILE))


def apply_tiles(diag_part, offd_part, own_rows, picked):
    own_rows = own_rows.reshape(own_rows.shape[0], LOADS, TILE)
    picked = picked.reshape(picked.shape[0], picked.shape[1], LOADS, TILE)
    result = jnp.einsum("iab,ivb->iva", as_tiles(diag_part), own_rows, precision=highest)
    result = result + jnp.einsum("ikab,ikvb->iva", as_tiles(offd_part), picked, precision=highest)
    return result.reshape(result.shape[0], LOADS * TILE)


def prolong(prol, coarse_rows):
    coarse_rows = coarse_rows.reshape(coarse_rows.shape[0], LOADS, TILE)
    result = jnp.einsum("iab,ivb->iva", as_tiles(prol), coarse_rows, precision=highest)
    return result.reshape(result.shape[0], LOADS * TILE)


def transposed(prol, fine_rows):
    fine_rows = fine_rows.reshape(fine_rows.shape[0], LOADS, TILE)
    result = jnp.einsum("iab,iva->ivb", as_tiles(prol), fine_rows, precision=highest)
    return result.reshape(result.shape[0], LOADS * TILE)


def chebyshev(operate, solution, residual, degree, finish):
    center = 0.5 * (cheb_high + cheb_low)
    radius = 0.5 * (cheb_high - cheb_low)
    sigma_value = center / radius
    rho_now = 1.0 / sigma_value
    direction = residual / center
    solution = solution + direction
    for turn_index in range(degree - 1):
        residual = residual - operate(direction)
        rho_next = 1.0 / (2.0 * sigma_value - rho_now)
        direction = (rho_next * rho_now) * direction + (2.0 * rho_next / radius) * residual
        solution = solution + direction
        rho_now = rho_next
    if finish:
        residual = residual - operate(direction)
    return solution, residual


def pick_rows(source, index_rows):
    return source[index_rows]


def reference(right_side, ghost_rows, cols_one, diag_one, offd_one, prol_one, agg_one, cols_two, diag_two, offd_two, prol_two, agg_two, cols_three, diag_three, offd_three):
    width = LOADS * TILE
    pick = jax.vmap(pick_rows)

    def level_one(vector):
        blocks = vector.reshape(BLOCKS, ROWS, width)
        zero_block = jnp.zeros_like(blocks[:1])
        left_blocks = jnp.concatenate([zero_block, blocks[:-1]], 0)
        right_blocks = jnp.concatenate([blocks[1:], zero_block], 0)
        lists = ghost_rows.reshape(BLOCKS, 2, GHOST)
        windows = jnp.concatenate([pick(left_blocks, lists[:, 0]), blocks, pick(right_blocks, lists[:, 1])], 1)
        picked = pick(windows, cols_one.reshape(BLOCKS, ROWS * OFFD)).reshape(ROWS_ALL, OFFD, width)
        return apply_tiles(diag_one, offd_one, vector, picked)

    def level_two(vector):
        pairs = vector.reshape(PAIRS, ROWS, width)
        zero_pair = jnp.zeros_like(pairs[:1])
        left_pairs = jnp.concatenate([zero_pair, pairs[:-1]], 0)
        right_pairs = jnp.concatenate([pairs[1:], zero_pair], 0)
        windows = jnp.concatenate([left_pairs, pairs, right_pairs], 1)
        picked = pick(windows, cols_two.reshape(PAIRS, ROWS * OFFD)).reshape(HALF_ALL, OFFD, width)
        return apply_tiles(diag_two, offd_two, vector, picked)

    def level_three(vector):
        return apply_tiles(diag_three, offd_three, vector, vector[cols_three])

    smooth_one, res_one = chebyshev(level_one, jnp.zeros_like(right_side), right_side, DEGREE, True)
    terms_one = transposed(prol_one, res_one).reshape(PAIRS, 2 * ROWS, width)
    pair_agg = agg_one.reshape(PAIRS, 2 * ROWS)
    one_hot = (pair_agg[:, None, :] == jnp.arange(ROWS, dtype=jnp.int32)[None, :, None]).astype(jnp.float32)
    rhs_two = jnp.einsum("pgi,piw->pgw", one_hot, terms_one, precision=highest).reshape(HALF_ALL, width)

    smooth_two, res_two = chebyshev(level_two, jnp.zeros_like(rhs_two), rhs_two, DEGREE, True)
    terms_two = transposed(prol_two, res_two)
    coarse_hot = (agg_two[None, :] == jnp.arange(COARSE, dtype=jnp.int32)[:, None]).astype(jnp.float32)
    coarse_rhs = jnp.dot(coarse_hot, terms_two, precision=highest)

    coarse_solution = chebyshev(level_three, jnp.zeros_like(coarse_rhs), coarse_rhs, COARSE_DEGREE, False)[0]

    corrected_two = smooth_two + prolong(prol_two, coarse_solution[agg_two])
    smoothed_two = chebyshev(level_two, corrected_two, rhs_two - level_two(corrected_two), DEGREE, False)[0]

    pair_rows = jnp.repeat(smoothed_two.reshape(PAIRS, ROWS, width), 2, axis=0)
    lifted = pick(pair_rows, agg_one.reshape(BLOCKS, ROWS)).reshape(ROWS_ALL, width)
    corrected_one = smooth_one + prolong(prol_one, lifted)
    solution = chebyshev(level_one, corrected_one, right_side - level_one(corrected_one), DEGREE, False)[0]
    return solution, coarse_solution
```

```python
import functools

import jax
import jax.numpy as jnp
from jax import lax
from jax.experimental import pallas as pl
from jax.experimental.pallas import tpu as pltpu
from jax.sharding import PartitionSpec as P

MESH = pl.DeviceIdType.MESH
TILE = 64
LOADS = 8
ROWS = 96
HALF = 48
COARSE = 32
GHOST = 24
UNROLL = 8
CENTER = 5.0
RADIUS = 4.0
F32 = jnp.float32
BF16 = jnp.bfloat16


def chebyshev_steps(degree):
    sigma = CENTER / RADIUS
    rho, pairs = 1.0 / sigma, []
    for _ in range(degree - 1):
        rho_next = 1.0 / (2.0 * sigma - rho)
        pairs.append((rho_next * rho, 2.0 * rho_next / RADIUS))
        rho = rho_next
    return pairs


STEPS = chebyshev_steps(3)
COARSE_STEPS = chebyshev_steps(8)


def halves(u):
    high = u.astype(BF16).astype(F32)
    return jnp.concatenate([high, u - high], 0).astype(BF16)


def twice(out):
    total = out[:LOADS] + out[LOADS:]
    return jnp.concatenate([total, total], 1)


def apply_one(u, tile):
    return twice(
        lax.dot_general(halves(u), tile, (((1,), (1,)), ((), ())), preferred_element_type=F32)
    )


def apply_two(u, w, tiles):
    left = jnp.concatenate([halves(u), halves(w)], 1)
    return twice(
        lax.dot_general(left, tiles, (((1,), (1,)), ((), ())), preferred_element_type=F32)
    )


def apply_transposed(u, tile):
    out = lax.dot_general(
        halves(u)[:, :TILE], tile, (((1,), (0,)), ((), ())), preferred_element_type=F32
    )
    total = out[:LOADS] + out[LOADS:]
    return total + pltpu.roll(total, TILE, 1)


def rows_loop(count, compute, store):
    def step(turn, carry):
        base = turn * UNROLL
        results = [compute(base + j) for j in range(UNROLL)]
        for j in range(UNROLL):
            store(base + j, results[j])
        return carry

    lax.fori_loop(0, count // UNROLL, step, 0)


def kernel(
    groups,
    size,
    rhs_ref,
    to_left_ref,
    to_right_ref,
    cols_one,
    diag_one,
    offd_one,
    prol_one,
    agg_one,
    hot_one,
    cols_two,
    diag_two,
    offd_two,
    prol_two,
    agg_two,
    hot_two,
    cols_three,
    diag_three,
    offd_three,
    out_ref,
    coarse_ref,
    win_one,
    send_one,
    got_one,
    x_one,
    r_one,
    win_two,
    send_two,
    got_two,
    x_two,
    r_two,
    rhs_two,
    terms,
    part,
    half_in,
    pair_send,
    pair_in,
    pair_all,
    terms_two,
    coarse_part,
    gather_a,
    gather_b,
    total_c,
    full_c,
    d_three,
    r_three,
    send_sem_one,
    recv_sem_one,
    send_sem_two,
    recv_sem_two,
    half_sem,
    pair_sem,
    sem_a,
    sem_b,
    sem_c,
):
    g, e = lax.axis_index("grp"), lax.axis_index("dev")
    me = g * size + e
    last = groups * size - 1
    pair, h = me // 2, me % 2
    pairs = groups * size // 2
    has_left, has_right = me > 0, me < last
    has_prev, has_next = pair > 0, pair < pairs - 1
    share = COARSE // size

    def at(index):
        return (index // size, index % size)

    lanes = lax.broadcasted_iota(jnp.int32, (LOADS, 2 * TILE), 1)
    low = lanes < TILE

    def unpack(packed):
        turned = pltpu.roll(packed, TILE, 1)
        return jnp.where(low, packed, turned), jnp.where(low, turned, packed)

    barrier = pltpu.get_barrier_semaphore()

    def greet(device):
        pl.semaphore_signal(barrier, inc=1, device_id=device, device_id_type=MESH)

    for k in range(1, size):
        greet((g, (e + k) % size))
    for k in range(1, groups):
        greet(((g + k) % groups, e))

    @pl.when(has_left)
    def _():
        greet(at(me - 1))

    @pl.when(has_right)
    def _():
        greet(at(me + 1))

    @pl.when(has_prev)
    def _():
        greet(at(2 * pair - 2))
        greet(at(2 * pair - 1))

    @pl.when(has_next)
    def _():
        greet(at(2 * pair + 2))
        greet(at(2 * pair + 3))

    def one(flag):
        return flag.astype(jnp.int32)

    expected = size - 1 + groups - 1 + one(has_left) + one(has_right)
    pl.semaphore_wait(barrier, expected + 2 * one(has_prev) + 2 * one(has_next))

    def level_one(s, store):
        def copy(side):
            target = at(me - 1) if side == 0 else at(me + 1)
            return pltpu.make_async_remote_copy(
                src_ref=send_one.at[s, side],
                dst_ref=got_one.at[s, 1 - side],
                send_sem=send_sem_one.at[s, side],
                recv_sem=recv_sem_one.at[s, 1 - side],
                device_id=target,
                device_id_type=MESH,
            )

        flags = (has_left, has_right)
        for side, rows in ((0, to_left_ref), (1, to_right_ref)):

            @pl.when(flags[side])
            def _(side=side, rows=rows):
                for t in range(GHOST // 2):
                    first = win_one[s, GHOST + rows[t]]
                    second = win_one[s, GHOST + rows[t + GHOST // 2]]
                    send_one[s, side, t] = jnp.where(low, first, second)
                copy(side).start()

        def diag(i):
            return r_one[i] - apply_one(win_one[s, GHOST + i], diag_one[i])

        def keep(i, value):
            r_one[i] = value

        rows_loop(ROWS, diag, keep)
        for side in range(2):
            base = 0 if side == 0 else GHOST + ROWS

            @pl.when(flags[side])
            def _(side=side, base=base):
                copy(1 - side).wait_recv()
                copy(side).wait_send()
                for t in range(GHOST // 2):
                    first, second = unpack(got_one[s, side, t])
                    win_one[s, base + t] = first
                    win_one[s, base + t + GHOST // 2] = second

            @pl.when(jnp.logical_not(flags[side]))
            def _(base=base):
                win_one[s, base : base + GHOST] = jnp.zeros((GHOST, LOADS, 2 * TILE), F32)

        def offd(i):
            return r_one[i] - apply_two(
                win_one[s, cols_one[i, 0]], win_one[s, cols_one[i, 1]], offd_one[i]
            )

        rows_loop(ROWS, offd, store)

    def level_two(s, store):
        own = ROWS + HALF * h

        def copy(target, slot):
            return pltpu.make_async_remote_copy(
                src_ref=send_two.at[s],
                dst_ref=got_two.at[s, slot],
                send_sem=send_sem_two.at[s, target_index[0]],
                recv_sem=recv_sem_two.at[s, slot],
                device_id=at(target),
                device_id_type=MESH,
            )

        target_index = [0]

        def make(number, target, slot):
            target_index[0] = number
            return copy(target, slot)

        for t in range(HALF // 2):
            send_two[s, t] = jnp.where(
                low, win_two[s, own + t], win_two[s, own + t + HALF // 2]
            )

        def prev_copies():
            return [make(y, 2 * pair - 2 + y, 3 + h) for y in range(2)]

        def next_copies():
            return [make(3 + y, 2 * pair + 2 + y, h) for y in range(2)]

        def partner_copy():
            return make(2, me + 1 - 2 * h, 2)

        @pl.when(has_prev)
        def _():
            for c in prev_copies():
                c.start()

        @pl.when(has_next)
        def _():
            for c in next_copies():
                c.start()

        partner_copy().start()

        def diag(j):
            return r_two[j] - apply_one(win_two[s, own + j], diag_two[j])

        def keep(j, value):
            r_two[j] = value

        rows_loop(HALF, diag, keep)

        def take(slot, base):
            for t in range(HALF // 2):
                first, second = unpack(got_two[s, slot, t])
                win_two[s, base + t] = first
                win_two[s, base + t + HALF // 2] = second

        partner_copy().wait()
        take(2, ROWS + HALF * (1 - h))

        @pl.when(has_prev)
        def _():
            for y, c in enumerate(prev_copies()):
                c.wait_send()
                make(y, 2 * pair - 2 + y, y).wait_recv()
                take(y, HALF * y)

        @pl.when(jnp.logical_not(has_prev))
        def _():
            win_two[s, 0:ROWS] = jnp.zeros((ROWS, LOADS, 2 * TILE), F32)

        @pl.when(has_next)
        def _():
            for y, c in enumerate(next_copies()):
                c.wait_send()
                make(3 + y, 2 * pair + 2 + y, 3 + y).wait_recv()
                take(3 + y, 2 * ROWS + HALF * y)

        @pl.when(jnp.logical_not(has_next))
        def _():
            win_two[s, 2 * ROWS : 3 * ROWS] = jnp.zeros((ROWS, LOADS, 2 * TILE), F32)

        def offd(j):
            return r_two[j] - apply_two(
                win_two[s, cols_two[j, 0]], win_two[s, cols_two[j, 1]], offd_two[j]
            )

        rows_loop(HALF, offd, store)

    for i in range(ROWS):
        value = rhs_ref[i]
        r_one[i] = value
        win_one[0, GHOST + i] = value / CENTER
        x_one[i] = value / CENTER

    def smooth_one(s, step):
        old, new = STEPS[step]

        def store(i, value):
            r_one[i] = value
            turn = old * win_one[s, GHOST + i] + new * value
            win_one[s + 1, GHOST + i] = turn
            x_one[i] = x_one[i] + turn

        level_one(s, store)

    def keep_one(i, value):
        r_one[i] = value

    smooth_one(0, 0)
    smooth_one(1, 1)
    level_one(2, keep_one)

    def restrict_one(i, value):
        terms[pl.ds(pl.multiple_of(i * LOADS, LOADS), LOADS), :] = value

    rows_loop(ROWS, lambda i: apply_transposed(r_one[i], prol_one[i]), restrict_one)

    def gathered(hot_ref, terms_ref, part_ref, count, fine):
        hot = hot_ref[...]
        wide = lax.broadcasted_iota(jnp.int32, (fine, 2 * TILE), 1) < TILE
        for v in range(LOADS):
            value = terms_ref[pl.ds(v, fine, stride=LOADS), :]
            high = value.astype(BF16).astype(F32)
            mixed = jnp.where(wide, high, value - high).astype(BF16)
            out = jnp.dot(hot, mixed, preferred_element_type=F32)
            part_ref[pl.ds(v, count, stride=LOADS), :] = out + pltpu.roll(out, TILE, 1)

    gathered(hot_one, terms, part, ROWS, ROWS)

    partner = at(me + 1 - 2 * h)
    mine, theirs = HALF * LOADS * h, HALF * LOADS * (1 - h)

    def part_rows(base, j):
        return part[pl.ds(pl.multiple_of(base + j * LOADS, LOADS), LOADS), :]

    for t in range(HALF // 2):
        pair_send[0, t] = jnp.where(
            low, part_rows(theirs, t), part_rows(theirs, t + HALF // 2)
        )
    half_copy = pltpu.make_async_remote_copy(
        src_ref=pair_send.at[0],
        dst_ref=half_in,
        send_sem=half_sem.at[0],
        recv_sem=half_sem.at[1],
        device_id=partner,
        device_id_type=MESH,
    )
    half_copy.start()
    half_copy.wait()
    own = ROWS + HALF * h
    for t in range(HALF // 2):
        for j, other in zip((t, t + HALF // 2), unpack(half_in[t])):
            value = part_rows(mine, j) + other
            rhs_two[j] = value
            r_two[j] = value
            win_two[0, own + j] = value / CENTER
            x_two[j] = value / CENTER

    def smooth_two(s, step):
        old, new = STEPS[step]

        def store(j, value):
            r_two[j] = value
            turn = old * win_two[s, own + j] + new * value
            x_two[j] = x_two[j] + turn
            win_two[s + 1, own + j] = turn

        level_two(s, store)

    def keep_two(j, value):
        r_two[j] = value

    smooth_two(0, 0)
    smooth_two(1, 1)
    level_two(2, keep_two)

    def restrict_two(j, value):
        terms_two[pl.ds(pl.multiple_of(j * LOADS, LOADS), LOADS), :] = value

    rows_loop(HALF, lambda j: apply_transposed(r_two[j], prol_two[j]), restrict_two)
    gathered(hot_two, terms_two, coarse_part, COARSE, HALF)

    width = share * LOADS

    def rows_of(member):
        return pl.ds(pl.multiple_of(member * width, LOADS), width)

    def copy_a(k):
        target = (e + k) % size
        return pltpu.make_async_remote_copy(
            src_ref=coarse_part.at[rows_of(target)],
            dst_ref=gather_a.at[k],
            send_sem=sem_a.at[0, k],
            recv_sem=sem_a.at[1, k],
            device_id=(g, target),
            device_id_type=MESH,
        )

    for k in range(1, size):
        copy_a(k).start()
    total = coarse_part[rows_of(e), :]
    for k in range(1, size):
        copy_a(k).wait()
        total = total + gather_a[k]
    gather_b[g] = total

    def copy_b(k, member):
        return pltpu.make_async_remote_copy(
            src_ref=gather_b.at[g],
            dst_ref=gather_b.at[member],
            send_sem=sem_b.at[0, k],
            recv_sem=sem_b.at[1, k],
            device_id=((g + k) % groups, e),
            device_id_type=MESH,
        )

    for k in range(1, groups):
        copy_b(k, g).start()
    for k in range(1, groups):
        copy_b(k, g).wait_send()
        copy_b(k, (g + groups - k) % groups).wait_recv()
    total = gather_b[0]
    for k in range(1, groups):
        total = total + gather_b[k]
    full_c[rows_of(e), :] = total

    def copy_c(k, member):
        return pltpu.make_async_remote_copy(
            src_ref=full_c.at[rows_of(e)],
            dst_ref=full_c.at[rows_of(member)],
            send_sem=sem_c.at[0, k],
            recv_sem=sem_c.at[1, k],
            device_id=(g, (e + k) % size),
            device_id_type=MESH,
        )

    for k in range(1, size):
        copy_c(k, e).start()
    for k in range(1, size):
        copy_c(k, e).wait_send()
        copy_c(k, (e + size - k) % size).wait_recv()

    for c in range(COARSE):
        value = full_c[c * LOADS : (c + 1) * LOADS, :]
        r_three[c] = value
        d_three[0, c] = value / CENTER
        coarse_ref[c] = value / CENTER

    for s, (old, new) in enumerate(COARSE_STEPS):
        now, later = s % 2, 1 - s % 2

        def coarse(c, now=now):
            return (
                r_three[c]
                - apply_one(d_three[now, c], diag_three[c])
                - apply_two(
                    d_three[now, cols_three[c, 0]],
                    d_three[now, cols_three[c, 1]],
                    offd_three[c],
                )
            )

        def store(c, value, now=now, later=later, old=old, new=new):
            r_three[c] = value
            turn = old * d_three[now, c] + new * value
            d_three[later, c] = turn
            coarse_ref[c] = coarse_ref[c] + turn

        rows_loop(COARSE, coarse, store)

    def corrected_two(j):
        return x_two[j] + apply_one(coarse_ref[agg_two[j]], prol_two[j])

    def store_two(j, value):
        x_two[j] = value
        r_two[j] = rhs_two[j]
        win_two[3, own + j] = value

    rows_loop(HALF, corrected_two, store_two)

    def first_two(j, value):
        r_two[j] = value
        turn = value / CENTER
        win_two[4, own + j] = turn
        x_two[j] = x_two[j] + turn

    level_two(3, first_two)
    smooth_two(4, 0)

    def last_two(j, value):
        turn = STEPS[1][0] * win_two[5, own + j] + STEPS[1][1] * value
        pair_all[HALF * h + j] = x_two[j] + turn

    level_two(5, last_two)
    for t in range(HALF // 2):
        pair_send[1, t] = jnp.where(
            low, pair_all[HALF * h + t], pair_all[HALF * h + t + HALF // 2]
        )
    pair_copy = pltpu.make_async_remote_copy(
        src_ref=pair_send.at[1],
        dst_ref=pair_in,
        send_sem=pair_sem.at[0],
        recv_sem=pair_sem.at[1],
        device_id=partner,
        device_id_type=MESH,
    )
    pair_copy.start()
    pair_copy.wait()
    for t in range(HALF // 2):
        first, second = unpack(pair_in[t])
        pair_all[HALF * (1 - h) + t] = first
        pair_all[HALF * (1 - h) + t + HALF // 2] = second

    def corrected_one(i):
        return x_one[i] + apply_one(pair_all[agg_one[i]], prol_one[i])

    def store_one(i, value):
        x_one[i] = value
        r_one[i] = rhs_ref[i]
        win_one[3, GHOST + i] = value

    rows_loop(ROWS, corrected_one, store_one)

    def first_one(i, value):
        r_one[i] = value
        turn = value / CENTER
        win_one[4, GHOST + i] = turn
        x_one[i] = x_one[i] + turn

    level_one(3, first_one)
    smooth_one(4, 0)

    def last_one(i, value):
        turn = STEPS[1][0] * win_one[5, GHOST + i] + STEPS[1][1] * value
        out_ref[i] = x_one[i] + turn

    level_one(5, last_one)


def split(tiles):
    high = lax.reduce_precision(tiles, 8, 7)
    return jnp.concatenate([high.astype(BF16), (tiles - high).astype(BF16)], -1)


def single(flat):
    return split(flat.reshape(flat.shape[0], TILE, TILE))


def double(flat):
    tiles = flat.reshape(flat.shape[0], 2, TILE, TILE)
    return jnp.concatenate([split(tiles[:, 0]), split(tiles[:, 1])], -1)


def body(
    groups,
    size,
    right_side,
    ghost_rows,
    cols_one,
    diag_one,
    offd_one,
    prol_one,
    agg_one,
    cols_two,
    diag_two,
    offd_two,
    prol_two,
    agg_two,
    cols_three,
    diag_three,
    offd_three,
):
    count = groups * size
    axes = ("grp", "dev")
    to_right = lax.ppermute(ghost_rows[0], axes, [(i + 1, i) for i in range(count - 1)])
    to_left = lax.ppermute(ghost_rows[1], axes, [(i, i + 1) for i in range(count - 1)])
    rhs = right_side.reshape(ROWS, LOADS, TILE)
    rhs = jnp.concatenate([rhs, rhs], -1)
    hot_one = (agg_one[None, :] == jnp.arange(ROWS, dtype=jnp.int32)[:, None]).astype(BF16)
    hot_two = (agg_two[None, :] == jnp.arange(COARSE, dtype=jnp.int32)[:, None]).astype(BF16)
    smem = pl.BlockSpec(memory_space=pltpu.SMEM)
    vmem = pl.BlockSpec(memory_space=pltpu.VMEM)
    row = (LOADS, 2 * TILE)
    share = COARSE // size
    dma = pltpu.SemaphoreType.DMA
    out, coarse = pl.pallas_call(
        functools.partial(kernel, groups, size),
        out_shape=(
            jax.ShapeDtypeStruct((ROWS, *row), F32),
            jax.ShapeDtypeStruct((COARSE, *row), F32),
        ),
        in_specs=[vmem, smem, smem]
        + [smem, vmem, vmem, vmem, smem, vmem] * 2
        + [smem, vmem, vmem],
        out_specs=(vmem, vmem),
        scratch_shapes=[
            pltpu.VMEM((6, ROWS + 2 * GHOST, *row), F32),
            pltpu.VMEM((6, 2, GHOST // 2, *row), F32),
            pltpu.VMEM((6, 2, GHOST // 2, *row), F32),
            pltpu.VMEM((ROWS, *row), F32),
            pltpu.VMEM((ROWS, *row), F32),
            pltpu.VMEM((6, 3 * ROWS, *row), F32),
            pltpu.VMEM((6, HALF // 2, *row), F32),
            pltpu.VMEM((6, 5, HALF // 2, *row), F32),
            pltpu.VMEM((HALF, *row), F32),
            pltpu.VMEM((HALF, *row), F32),
            pltpu.VMEM((HALF, *row), F32),
            pltpu.VMEM((ROWS * LOADS, 2 * TILE), F32),
            pltpu.VMEM((ROWS * LOADS, 2 * TILE), F32),
            pltpu.VMEM((HALF // 2, *row), F32),
            pltpu.VMEM((2, HALF // 2, *row), F32),
            pltpu.VMEM((HALF // 2, *row), F32),
            pltpu.VMEM((ROWS, *row), F32),
            pltpu.VMEM((HALF * LOADS, 2 * TILE), F32),
            pltpu.VMEM((COARSE * LOADS, 2 * TILE), F32),
            pltpu.VMEM((size, share * LOADS, 2 * TILE), F32),
            pltpu.VMEM((groups, share * LOADS, 2 * TILE), F32),
            pltpu.VMEM((share * LOADS, 2 * TILE), F32),
            pltpu.VMEM((COARSE * LOADS, 2 * TILE), F32),
            pltpu.VMEM((2, COARSE, *row), F32),
            pltpu.VMEM((COARSE, *row), F32),
            dma((6, 2)),
            dma((6, 2)),
            dma((6, 5)),
            dma((6, 5)),
            dma((2,)),
            dma((2,)),
            dma((2, size)),
            dma((2, groups)),
            dma((2, size)),
        ],
        compiler_params=pltpu.CompilerParams(
            collective_id=0, has_side_effects=True, vmem_limit_bytes=56 * 2**20
        ),
    )(
        rhs,
        to_left,
        to_right,
        cols_one,
        single(diag_one),
        double(offd_one),
        single(prol_one),
        agg_one,
        hot_one,
        cols_two,
        single(diag_two),
        double(offd_two),
        single(prol_two),
        agg_two,
        hot_two,
        cols_three,
        single(diag_three),
        double(offd_three),
    )
    return (
        out[:, :, :TILE].reshape(ROWS, LOADS * TILE),
        coarse[:, :, :TILE].reshape(COARSE, LOADS * TILE),
    )


def solution(mesh):
    groups, size = mesh.shape["grp"], mesh.shape["dev"]
    rows = P(("grp", "dev"), None)
    tiles = P(("grp", "dev"), None, None)
    flat = P(("grp", "dev"))
    return jax.shard_map(
        functools.partial(body, groups, size),
        mesh=mesh,
        in_specs=(
            rows,
            rows,
            rows,
            rows,
            tiles,
            rows,
            flat,
            rows,
            rows,
            tiles,
            rows,
            flat,
            P(),
            P(),
            P(),
        ),
        out_specs=(rows, P()),
        check_vma=False,
    )
```

```python
import functools

import jax
import jax.numpy as jnp
import numpy as np
from jax import lax
from jax.experimental import pallas as pl
from jax.experimental.pallas import tpu as pltpu
from jax.sharding import PartitionSpec as P

MESH = pl.DeviceIdType.MESH
TILE = 64
LOADS = 8
ROWS = 96
HALF = 48
COARSE = 32
GHOST = 24
UNROLL = 24
GROUP = 8
CENTER = 5.0
RADIUS = 4.0
F32 = jnp.float32
BF16 = jnp.bfloat16


def chebyshev_steps(degree):
    sigma = CENTER / RADIUS
    rho, pairs = 1.0 / sigma, []
    for _ in range(degree - 1):
        rho_next = 1.0 / (2.0 * sigma - rho)
        pairs.append((rho_next * rho, 2.0 * rho_next / RADIUS))
        rho = rho_next
    return pairs


def spread():
    order = np.concatenate([np.arange(0, TILE, 2), np.arange(1, TILE, 2)])
    move = np.zeros((TILE, TILE), np.float32)
    move[order, np.arange(TILE)] = 1.0
    tiles = np.zeros((2, 2, TILE, 2, 2, TILE), np.float32)
    for part in range(2):
        for parity in range(2):
            tiles[part, parity, :, parity, part, :] = move
    enter = np.zeros((2, 2, TILE, 2, TILE), np.float32)
    leave = np.zeros((2, TILE, 2, TILE), np.float32)
    for half in range(2):
        enter[half, half, :, 0] = enter[half, half, :, 1] = move
        leave[half, :, half] = move.T
    rows = np.concatenate([enter.reshape(4 * TILE, -1), leave.reshape(2 * TILE, -1)])
    return tiles.reshape(4 * TILE, 4 * TILE), rows.reshape(3, 2 * TILE, 2 * TILE)


STEPS = chebyshev_steps(3)
COARSE_STEPS = chebyshev_steps(8)


def halves(u):
    high = u.astype(BF16).astype(F32)
    return jnp.concatenate([high, u - high], 0).astype(BF16)


def twice(out):
    total = out[:LOADS] + out[LOADS:]
    return jnp.concatenate([total, total], 1)


def apply_one(u, tile):
    return twice(
        lax.dot_general(halves(u), tile, (((1,), (1,)), ((), ())), preferred_element_type=F32)
    )


def apply_two(u, w, tiles):
    left = jnp.concatenate([halves(u), halves(w)], 1)
    return twice(
        lax.dot_general(left, tiles, (((1,), (1,)), ((), ())), preferred_element_type=F32)
    )


def apply_transposed(u, tile):
    out = lax.dot_general(
        halves(u)[:, :TILE], tile, (((1,), (0,)), ((), ())), preferred_element_type=F32
    )
    total = out[:LOADS] + out[LOADS:]
    return total + pltpu.roll(total, TILE, 1)


def rows_loop(count, compute, store, unroll=UNROLL):
    def step(turn, carry):
        base = turn * unroll
        results = [compute(base + j) for j in range(unroll)]
        for j in range(unroll):
            store(base + j, results[j])
        return carry

    lax.fori_loop(0, count // unroll, step, 0)


def exact_dot(value, matrix):
    high = value.astype(BF16)
    rest = value - high.astype(F32)
    middle = rest.astype(BF16)
    small = (rest - middle.astype(F32)).astype(BF16)
    first, second, third = (
        jnp.dot(part, matrix, preferred_element_type=F32) for part in (high, middle, small)
    )
    return first + second + third


def converted(tiles, matrix):
    value = jnp.concatenate(tiles, 0)
    high = value.astype(BF16)
    small = (value - high.astype(F32)).astype(BF16)
    both = jnp.concatenate([high, small], 1)
    return jnp.dot(both, matrix, preferred_element_type=F32).astype(BF16)


def keep_tile(ref, i, lanes, rows):
    ref[i, : TILE // 2, lanes] = rows[:, : 2 * TILE]
    ref[i, TILE // 2 :, lanes] = rows[:, 2 * TILE :]


def convert_single(raw, ref, matrix, count):
    def step(turn, carry):
        base = pl.multiple_of(turn * GROUP * TILE // 2, GROUP * TILE // 2)
        tiles = [raw[pl.ds(base + j, TILE // 2, stride=GROUP), :] for j in range(GROUP)]
        out = converted(tiles, matrix[...])
        for j in range(GROUP):
            rows = out[j * TILE // 2 : (j + 1) * TILE // 2]
            keep_tile(ref, turn * GROUP + j, slice(0, 2 * TILE), rows)
        return carry

    lax.fori_loop(0, count // GROUP, step, 0)


def convert_double(raw, ref, matrix, count):
    def step(turn, carry):
        base = pl.multiple_of(turn * GROUP * TILE // 2, GROUP * TILE // 2)
        tiles = [
            raw[pl.ds(base + j * TILE + k, TILE // 2, stride=2), :]
            for j in range(GROUP // 2)
            for k in range(2)
        ]
        out = converted(tiles, matrix[...])
        for j in range(GROUP // 2):
            for k in range(2):
                place = 2 * j + k
                rows = out[place * TILE // 2 : (place + 1) * TILE // 2]
                lanes = slice(2 * TILE * k, 2 * TILE * (k + 1))
                keep_tile(ref, turn * (GROUP // 2) + j, lanes, rows)
        return carry

    lax.fori_loop(0, count // (GROUP // 2), step, 0)


def kernel(
    groups,
    size,
    matrix,
    moves,
    rhs_in,
    ghost_rows,
    cols_one,
    diag_one_raw,
    offd_one_raw,
    prol_one_raw,
    agg_one,
    hot_one,
    cols_two,
    diag_two_raw,
    offd_two_raw,
    prol_two_raw,
    agg_two,
    hot_two,
    cols_three,
    diag_three_raw,
    offd_three_raw,
    out_ref,
    coarse_out,
    *scratch,
):
    raws = (
        diag_one_raw,
        offd_one_raw,
        prol_one_raw,
        diag_two_raw,
        offd_two_raw,
        prol_two_raw,
        diag_three_raw,
        offd_three_raw,
    )
    staged, tiles, scratch = scratch[:8], scratch[8:16], scratch[16:]
    diag_one, offd_one, prol_one, diag_two, offd_two, prol_two, diag_three, offd_three = tiles
    (
        rhs_one,
        win_one,
        send_one,
        got_one,
        x_one,
        r_one,
        win_two,
        send_two,
        got_two,
        x_two,
        r_two,
        rhs_two,
        terms,
        part,
        half_in,
        pair_send,
        pair_in,
        pair_all,
        terms_two,
        coarse_part,
        gather_a,
        gather_b,
        full_c,
        d_three,
        r_three,
        coarse_ref,
        lists_in,
        lists,
        stage_sem,
        list_sem,
        send_sem_one,
        recv_sem_one,
        send_sem_two,
        recv_sem_two,
        half_sem,
        pair_sem,
        sem_a,
        sem_b,
        sem_c,
    ) = scratch
    stages = [
        pltpu.make_async_copy(raws[k], staged[k], stage_sem.at[k]) for k in range(8)
    ]
    for stage in stages:
        stage.start()

    def prepare(k, convert, count):
        stages[k].wait()
        convert(staged[k], tiles[k], matrix, count)

    g, e = lax.axis_index("grp"), lax.axis_index("dev")
    me = g * size + e
    last = groups * size - 1
    pair, h = me // 2, me % 2
    pairs = groups * size // 2
    has_left, has_right = me > 0, me < last
    has_prev, has_next = pair > 0, pair < pairs - 1
    share = COARSE // size

    def at(index):
        return (index // size, index % size)

    lanes = lax.broadcasted_iota(jnp.int32, (LOADS, 2 * TILE), 1)
    low = lanes < TILE

    def unpack(packed):
        turned = pltpu.roll(packed, TILE, 1)
        return jnp.where(low, packed, turned), jnp.where(low, turned, packed)

    barrier = pltpu.get_barrier_semaphore()

    def greet(device):
        pl.semaphore_signal(barrier, inc=1, device_id=device, device_id_type=MESH)

    for k in range(1, size):
        greet((g, (e + k) % size))
    for k in range(1, groups):
        greet(((g + k) % groups, e))

    @pl.when(has_left)
    def _():
        greet(at(me - 1))

    @pl.when(has_right)
    def _():
        greet(at(me + 1))

    @pl.when(has_prev)
    def _():
        greet(at(2 * pair - 2))
        greet(at(2 * pair - 1))

    @pl.when(has_next)
    def _():
        greet(at(2 * pair + 2))
        greet(at(2 * pair + 3))

    def one(flag):
        return flag.astype(jnp.int32)

    expected = size - 1 + groups - 1 + one(has_left) + one(has_right)
    pl.semaphore_wait(barrier, expected + 2 * one(has_prev) + 2 * one(has_next))

    def list_copy(side):
        return pltpu.make_async_remote_copy(
            src_ref=ghost_rows,
            dst_ref=lists_in.at[1 - side],
            send_sem=list_sem.at[0, side],
            recv_sem=list_sem.at[1, 1 - side],
            device_id=at(me - 1) if side == 0 else at(me + 1),
            device_id_type=MESH,
        )

    for side, flag in ((0, has_left), (1, has_right)):

        @pl.when(flag)
        def _(side=side):
            list_copy(side).start()

    for q in range(LOADS // 2):
        value = rhs_in[:, 2 * TILE * q : 2 * TILE * (q + 1)]
        for half in range(2):
            rhs_one[pl.ds(2 * q + half, ROWS, stride=LOADS), :] = exact_dot(value, moves[half])

    def rhs_row(i):
        return rhs_one[pl.ds(pl.multiple_of(i * LOADS, LOADS), LOADS), :]

    for side, flag in ((0, has_left), (1, has_right)):

        @pl.when(flag)
        def _(side=side):
            list_copy(1 - side).wait_recv()
            list_copy(side).wait_send()
            local = pltpu.make_async_copy(
                lists_in.at[side], lists.at[side], list_sem.at[2, side]
            )
            local.start()
            local.wait()

    def level_one(s, store, before=None, during=None):
        def copy(side):
            target = at(me - 1) if side == 0 else at(me + 1)
            return pltpu.make_async_remote_copy(
                src_ref=send_one.at[s, side],
                dst_ref=got_one.at[s, 1 - side],
                send_sem=send_sem_one.at[s, side],
                recv_sem=recv_sem_one.at[s, 1 - side],
                device_id=target,
                device_id_type=MESH,
            )

        flags = (has_left, has_right)
        for side in range(2):

            @pl.when(flags[side])
            def _(side=side):
                for t in range(GHOST // 2):
                    first = win_one[s, GHOST + lists[side, 1 - side, t]]
                    second = win_one[s, GHOST + lists[side, 1 - side, t + GHOST // 2]]
                    send_one[s, side, t] = jnp.where(low, first, second)
                copy(side).start()

        if before:
            before()

        def diag(i):
            return r_one[i] - apply_one(win_one[s, GHOST + i], diag_one[i])

        def keep(i, value):
            r_one[i] = value

        rows_loop(ROWS, diag, keep)
        if during:
            during()
        for side in range(2):
            base = 0 if side == 0 else GHOST + ROWS

            @pl.when(flags[side])
            def _(side=side, base=base):
                copy(1 - side).wait_recv()
                copy(side).wait_send()
                for t in range(GHOST // 2):
                    first, second = unpack(got_one[s, side, t])
                    win_one[s, base + t] = first
                    win_one[s, base + t + GHOST // 2] = second

            @pl.when(jnp.logical_not(flags[side]))
            def _(base=base):
                win_one[s, base : base + GHOST] = jnp.zeros((GHOST, LOADS, 2 * TILE), F32)

        def offd(i):
            return r_one[i] - apply_two(
                win_one[s, cols_one[i, 0]], win_one[s, cols_one[i, 1]], offd_one[i]
            )

        rows_loop(ROWS, offd, store)

    def level_two(s, store, during=None):
        own = ROWS + HALF * h

        def copy(target, slot):
            return pltpu.make_async_remote_copy(
                src_ref=send_two.at[s],
                dst_ref=got_two.at[s, slot],
                send_sem=send_sem_two.at[s, target_index[0]],
                recv_sem=recv_sem_two.at[s, slot],
                device_id=at(target),
                device_id_type=MESH,
            )

        target_index = [0]

        def make(number, target, slot):
            target_index[0] = number
            return copy(target, slot)

        for t in range(HALF // 2):
            send_two[s, t] = jnp.where(
                low, win_two[s, own + t], win_two[s, own + t + HALF // 2]
            )

        def prev_copies():
            return [make(y, 2 * pair - 2 + y, 3 + h) for y in range(2)]

        def next_copies():
            return [make(3 + y, 2 * pair + 2 + y, h) for y in range(2)]

        def partner_copy():
            return make(2, me + 1 - 2 * h, 2)

        @pl.when(has_prev)
        def _():
            for c in prev_copies():
                c.start()

        @pl.when(has_next)
        def _():
            for c in next_copies():
                c.start()

        partner_copy().start()

        def diag(j):
            return r_two[j] - apply_one(win_two[s, own + j], diag_two[j])

        def keep(j, value):
            r_two[j] = value

        rows_loop(HALF, diag, keep)
        if during:
            during()

        def take(slot, base):
            for t in range(HALF // 2):
                first, second = unpack(got_two[s, slot, t])
                win_two[s, base + t] = first
                win_two[s, base + t + HALF // 2] = second

        partner_copy().wait()
        take(2, ROWS + HALF * (1 - h))

        @pl.when(has_prev)
        def _():
            for y, c in enumerate(prev_copies()):
                c.wait_send()
                make(y, 2 * pair - 2 + y, y).wait_recv()
                take(y, HALF * y)

        @pl.when(jnp.logical_not(has_prev))
        def _():
            win_two[s, 0:ROWS] = jnp.zeros((ROWS, LOADS, 2 * TILE), F32)

        @pl.when(has_next)
        def _():
            for y, c in enumerate(next_copies()):
                c.wait_send()
                make(3 + y, 2 * pair + 2 + y, 3 + y).wait_recv()
                take(3 + y, 2 * ROWS + HALF * y)

        @pl.when(jnp.logical_not(has_next))
        def _():
            win_two[s, 2 * ROWS : 3 * ROWS] = jnp.zeros((ROWS, LOADS, 2 * TILE), F32)

        def offd(j):
            return r_two[j] - apply_two(
                win_two[s, cols_two[j, 0]], win_two[s, cols_two[j, 1]], offd_two[j]
            )

        rows_loop(HALF, offd, store)

    for i in range(ROWS):
        value = rhs_row(i)
        r_one[i] = value
        win_one[0, GHOST + i] = value / CENTER
        x_one[i] = value / CENTER

    def smooth_one(s, step, before=None, during=None):
        old, new = STEPS[step]

        def store(i, value):
            r_one[i] = value
            turn = old * win_one[s, GHOST + i] + new * value
            win_one[s + 1, GHOST + i] = turn
            x_one[i] = x_one[i] + turn

        level_one(s, store, before, during)

    def keep_one(i, value):
        r_one[i] = value

    def prepare_prol_one():
        prepare(2, convert_single, ROWS)
        prepare(3, convert_single, HALF)

    smooth_one(
        0,
        0,
        lambda: prepare(0, convert_single, ROWS),
        lambda: prepare(1, convert_double, ROWS),
    )
    smooth_one(1, 1, None, prepare_prol_one)
    level_one(2, keep_one, None, lambda: prepare(4, convert_double, HALF))

    def restrict_one(i, value):
        terms[pl.ds(pl.multiple_of(i * LOADS, LOADS), LOADS), :] = value

    rows_loop(ROWS, lambda i: apply_transposed(r_one[i], prol_one[i]), restrict_one)

    def gathered(hot_ref, terms_ref, part_ref, count, fine):
        hot = hot_ref[...]
        wide = lax.broadcasted_iota(jnp.int32, (fine, 2 * TILE), 1) < TILE
        for v in range(LOADS):
            value = terms_ref[pl.ds(v, fine, stride=LOADS), :]
            high = value.astype(BF16).astype(F32)
            mixed = jnp.where(wide, high, value - high).astype(BF16)
            out = jnp.dot(hot, mixed, preferred_element_type=F32)
            part_ref[pl.ds(v, count, stride=LOADS), :] = out + pltpu.roll(out, TILE, 1)

    gathered(hot_one, terms, part, ROWS, ROWS)

    partner = at(me + 1 - 2 * h)
    mine, theirs = HALF * LOADS * h, HALF * LOADS * (1 - h)

    def part_rows(base, j):
        return part[pl.ds(pl.multiple_of(base + j * LOADS, LOADS), LOADS), :]

    for t in range(HALF // 2):
        pair_send[0, t] = jnp.where(
            low, part_rows(theirs, t), part_rows(theirs, t + HALF // 2)
        )
    half_copy = pltpu.make_async_remote_copy(
        src_ref=pair_send.at[0],
        dst_ref=half_in,
        send_sem=half_sem.at[0],
        recv_sem=half_sem.at[1],
        device_id=partner,
        device_id_type=MESH,
    )
    half_copy.start()
    half_copy.wait()
    own = ROWS + HALF * h
    for t in range(HALF // 2):
        for j, other in zip((t, t + HALF // 2), unpack(half_in[t])):
            value = part_rows(mine, j) + other
            rhs_two[j] = value
            r_two[j] = value
            win_two[0, own + j] = value / CENTER
            x_two[j] = value / CENTER

    def smooth_two(s, step, during=None):
        old, new = STEPS[step]

        def store(j, value):
            r_two[j] = value
            turn = old * win_two[s, own + j] + new * value
            x_two[j] = x_two[j] + turn
            win_two[s + 1, own + j] = turn

        level_two(s, store, during)

    def keep_two(j, value):
        r_two[j] = value

    smooth_two(0, 0, lambda: prepare(5, convert_single, HALF))
    smooth_two(1, 1, lambda: prepare(6, convert_single, COARSE))
    level_two(2, keep_two, lambda: prepare(7, convert_double, COARSE))

    def restrict_two(j, value):
        terms_two[pl.ds(pl.multiple_of(j * LOADS, LOADS), LOADS), :] = value

    rows_loop(HALF, lambda j: apply_transposed(r_two[j], prol_two[j]), restrict_two)
    gathered(hot_two, terms_two, coarse_part, COARSE, HALF)

    width = share * LOADS

    def rows_of(member):
        return pl.ds(pl.multiple_of(member * width, LOADS), width)

    def copy_a(k):
        target = (e + k) % size
        return pltpu.make_async_remote_copy(
            src_ref=coarse_part.at[rows_of(target)],
            dst_ref=gather_a.at[k],
            send_sem=sem_a.at[0, k],
            recv_sem=sem_a.at[1, k],
            device_id=(g, target),
            device_id_type=MESH,
        )

    for k in range(1, size):
        copy_a(k).start()
    total = coarse_part[rows_of(e), :]
    for k in range(1, size):
        copy_a(k).wait()
        total = total + gather_a[k]
    gather_b[g] = total

    def copy_b(k, member):
        return pltpu.make_async_remote_copy(
            src_ref=gather_b.at[g],
            dst_ref=gather_b.at[member],
            send_sem=sem_b.at[0, k],
            recv_sem=sem_b.at[1, k],
            device_id=((g + k) % groups, e),
            device_id_type=MESH,
        )

    for k in range(1, groups):
        copy_b(k, g).start()
    for k in range(1, groups):
        copy_b(k, g).wait_send()
        copy_b(k, (g + groups - k) % groups).wait_recv()
    total = gather_b[0]
    for k in range(1, groups):
        total = total + gather_b[k]
    full_c[rows_of(e), :] = total

    def copy_c(k, member):
        return pltpu.make_async_remote_copy(
            src_ref=full_c.at[rows_of(e)],
            dst_ref=full_c.at[rows_of(member)],
            send_sem=sem_c.at[0, k],
            recv_sem=sem_c.at[1, k],
            device_id=(g, (e + k) % size),
            device_id_type=MESH,
        )

    for k in range(1, size):
        copy_c(k, e).start()
    for k in range(1, size):
        copy_c(k, e).wait_send()
        copy_c(k, (e + size - k) % size).wait_recv()

    for c in range(COARSE):
        value = full_c[c * LOADS : (c + 1) * LOADS, :]
        r_three[c] = value
        d_three[0, c] = value / CENTER
        coarse_ref[c] = value / CENTER

    for s, (old, new) in enumerate(COARSE_STEPS):
        now, later = s % 2, 1 - s % 2

        def coarse(c, now=now):
            return (
                r_three[c]
                - apply_one(d_three[now, c], diag_three[c])
                - apply_two(
                    d_three[now, cols_three[c, 0]],
                    d_three[now, cols_three[c, 1]],
                    offd_three[c],
                )
            )

        def store(c, value, now=now, later=later, old=old, new=new):
            r_three[c] = value
            turn = old * d_three[now, c] + new * value
            d_three[later, c] = turn
            coarse_ref[c] = coarse_ref[c] + turn

        rows_loop(COARSE, coarse, store, 16)

    def corrected_two(j):
        return x_two[j] + apply_one(coarse_ref[agg_two[j]], prol_two[j])

    def store_two(j, value):
        x_two[j] = value
        r_two[j] = rhs_two[j]
        win_two[3, own + j] = value

    rows_loop(HALF, corrected_two, store_two)

    def first_two(j, value):
        r_two[j] = value
        turn = value / CENTER
        win_two[4, own + j] = turn
        x_two[j] = x_two[j] + turn

    level_two(3, first_two)
    smooth_two(4, 0)

    def last_two(j, value):
        turn = STEPS[1][0] * win_two[5, own + j] + STEPS[1][1] * value
        pair_all[HALF * h + j] = x_two[j] + turn

    level_two(5, last_two)
    for t in range(HALF // 2):
        pair_send[1, t] = jnp.where(
            low, pair_all[HALF * h + t], pair_all[HALF * h + t + HALF // 2]
        )
    pair_copy = pltpu.make_async_remote_copy(
        src_ref=pair_send.at[1],
        dst_ref=pair_in,
        send_sem=pair_sem.at[0],
        recv_sem=pair_sem.at[1],
        device_id=partner,
        device_id_type=MESH,
    )
    pair_copy.start()
    pair_copy.wait()
    for t in range(HALF // 2):
        first, second = unpack(pair_in[t])
        pair_all[HALF * (1 - h) + t] = first
        pair_all[HALF * (1 - h) + t + HALF // 2] = second

    def corrected_one(i):
        return x_one[i] + apply_one(pair_all[agg_one[i]], prol_one[i])

    def store_one(i, value):
        x_one[i] = value
        r_one[i] = rhs_row(i)
        win_one[3, GHOST + i] = value

    rows_loop(ROWS, corrected_one, store_one)

    def first_one(i, value):
        r_one[i] = value
        turn = value / CENTER
        win_one[4, GHOST + i] = turn
        x_one[i] = x_one[i] + turn

    level_one(3, first_one)
    smooth_one(4, 0)

    def last_one(i, value):
        turn = STEPS[1][0] * win_one[5, GHOST + i] + STEPS[1][1] * value
        terms[pl.ds(pl.multiple_of(i * LOADS, LOADS), LOADS), :] = x_one[i] + turn

    level_one(5, last_one)

    def leave(stage_ref, target_ref, count):
        wide = lax.broadcasted_iota(jnp.int32, (count, 2 * TILE), 1) < TILE
        for q in range(LOADS // 2):
            first = stage_ref[pl.ds(2 * q, count, stride=LOADS), :]
            second = stage_ref[pl.ds(2 * q + 1, count, stride=LOADS), :]
            target_ref[:, 2 * TILE * q : 2 * TILE * (q + 1)] = exact_dot(
                jnp.where(wide, first, second), moves[2]
            )

    leave(terms, out_ref, ROWS)
    for c in range(COARSE):
        coarse_part[c * LOADS : (c + 1) * LOADS, :] = coarse_ref[c]
    leave(coarse_part, coarse_out, COARSE)


def single(flat):
    count = flat.shape[0]
    tiles = flat.reshape(count // GROUP, GROUP, TILE // 2, 2 * TILE)
    return tiles.transpose(0, 2, 1, 3).reshape(count * TILE // 2, 2 * TILE)


def double(flat):
    count = flat.shape[0]
    tiles = flat.reshape(count, 2, TILE // 2, 2 * TILE)
    return tiles.transpose(0, 2, 1, 3).reshape(count * TILE, 2 * TILE)


def body(
    groups,
    size,
    right_side,
    ghost_rows,
    cols_one,
    diag_one,
    offd_one,
    prol_one,
    agg_one,
    cols_two,
    diag_two,
    offd_two,
    prol_two,
    agg_two,
    cols_three,
    diag_three,
    offd_three,
):
    matrix, moves = (jnp.asarray(a, BF16) for a in spread())
    hot_one = (agg_one[None, :] == jnp.arange(ROWS, dtype=jnp.int32)[:, None]).astype(BF16)
    hot_two = (agg_two[None, :] == jnp.arange(COARSE, dtype=jnp.int32)[:, None]).astype(BF16)
    smem = pl.BlockSpec(memory_space=pltpu.SMEM)
    vmem = pl.BlockSpec(memory_space=pltpu.VMEM)
    row = (LOADS, 2 * TILE)
    share = COARSE // size
    dma = pltpu.SemaphoreType.DMA
    hbm = pl.BlockSpec(memory_space=pl.ANY)
    raw = [
        single(diag_one),
        double(offd_one),
        single(prol_one),
        single(diag_two),
        double(offd_two),
        single(prol_two),
        single(diag_three),
        double(offd_three),
    ]
    widths = [2, 4, 2, 2, 4, 2, 2, 4]
    counts = [ROWS] * 3 + [HALF] * 3 + [COARSE] * 2
    return pl.pallas_call(
        functools.partial(kernel, groups, size),
        out_shape=(
            jax.ShapeDtypeStruct((ROWS, LOADS * TILE), F32),
            jax.ShapeDtypeStruct((COARSE, LOADS * TILE), F32),
        ),
        in_specs=[vmem] * 4
        + [smem, hbm, hbm, hbm, smem, vmem] * 2
        + [smem, hbm, hbm],
        out_specs=(vmem, vmem),
        scratch_shapes=[pltpu.VMEM(a.shape, F32) for a in raw]
        + [pltpu.VMEM((n, TILE, w * TILE), BF16) for n, w in zip(counts, widths)]
        + [
            pltpu.VMEM((ROWS * LOADS, 2 * TILE), F32),
            pltpu.VMEM((6, ROWS + 2 * GHOST, *row), F32),
            pltpu.VMEM((6, 2, GHOST // 2, *row), F32),
            pltpu.VMEM((6, 2, GHOST // 2, *row), F32),
            pltpu.VMEM((ROWS, *row), F32),
            pltpu.VMEM((ROWS, *row), F32),
            pltpu.VMEM((6, 3 * ROWS, *row), F32),
            pltpu.VMEM((6, HALF // 2, *row), F32),
            pltpu.VMEM((6, 5, HALF // 2, *row), F32),
            pltpu.VMEM((HALF, *row), F32),
            pltpu.VMEM((HALF, *row), F32),
            pltpu.VMEM((HALF, *row), F32),
            pltpu.VMEM((ROWS * LOADS, 2 * TILE), F32),
            pltpu.VMEM((ROWS * LOADS, 2 * TILE), F32),
            pltpu.VMEM((HALF // 2, *row), F32),
            pltpu.VMEM((2, HALF // 2, *row), F32),
            pltpu.VMEM((HALF // 2, *row), F32),
            pltpu.VMEM((ROWS, *row), F32),
            pltpu.VMEM((HALF * LOADS, 2 * TILE), F32),
            pltpu.VMEM((COARSE * LOADS, 2 * TILE), F32),
            pltpu.VMEM((size, share * LOADS, 2 * TILE), F32),
            pltpu.VMEM((groups, share * LOADS, 2 * TILE), F32),
            pltpu.VMEM((COARSE * LOADS, 2 * TILE), F32),
            pltpu.VMEM((2, COARSE, *row), F32),
            pltpu.VMEM((COARSE, *row), F32),
            pltpu.VMEM((COARSE, *row), F32),
            pltpu.VMEM((2, 2, GHOST), jnp.int32),
            pltpu.SMEM((2, 2, GHOST), jnp.int32),
            dma((8,)),
            dma((3, 2)),
            dma((6, 2)),
            dma((6, 2)),
            dma((6, 5)),
            dma((6, 5)),
            dma((2,)),
            dma((2,)),
            dma((2, size)),
            dma((2, groups)),
            dma((2, size)),
        ],
        compiler_params=pltpu.CompilerParams(
            collective_id=0, has_side_effects=True, vmem_limit_bytes=56 * 2**20
        ),
    )(
        matrix,
        moves,
        right_side,
        ghost_rows,
        cols_one,
        *raw[:3],
        agg_one,
        hot_one,
        cols_two,
        *raw[3:6],
        agg_two,
        hot_two,
        cols_three,
        *raw[6:],
    )


def solution(mesh):
    groups, size = mesh.shape["grp"], mesh.shape["dev"]
    rows = P(("grp", "dev"), None)
    tiles = P(("grp", "dev"), None, None)
    flat = P(("grp", "dev"))
    return jax.shard_map(
        functools.partial(body, groups, size),
        mesh=mesh,
        in_specs=(
            rows,
            rows,
            rows,
            rows,
            tiles,
            rows,
            flat,
            rows,
            rows,
            tiles,
            rows,
            flat,
            P(),
            P(),
            P(),
        ),
        out_specs=(rows, P()),
        check_vma=False,
    )
```

```python
import functools

import jax
import jax.numpy as jnp
import numpy as np
from jax import lax
from jax.experimental import pallas as pl
from jax.experimental.pallas import tpu as pltpu
from jax.sharding import PartitionSpec as P

MESH = pl.DeviceIdType.MESH
TILE = 64
LOADS = 8
ROWS = 96
HALF = 48
COARSE = 32
GHOST = 24
UNROLL = 24
GROUP = 8
CENTER = 5.0
RADIUS = 4.0
F32 = jnp.float32
BF16 = jnp.bfloat16


def chebyshev_steps(degree):
    sigma = CENTER / RADIUS
    rho, pairs = 1.0 / sigma, []
    for _ in range(degree - 1):
        rho_next = 1.0 / (2.0 * sigma - rho)
        pairs.append((rho_next * rho, 2.0 * rho_next / RADIUS))
        rho = rho_next
    return pairs


def spread():
    order = np.concatenate([np.arange(0, TILE, 2), np.arange(1, TILE, 2)])
    move = np.zeros((TILE, TILE), np.float32)
    move[order, np.arange(TILE)] = 1.0
    tiles = np.zeros((2, 2, TILE, 2, 2, TILE), np.float32)
    for part in range(2):
        for parity in range(2):
            tiles[part, parity, :, parity, part, :] = move
    enter = np.zeros((2, 2, TILE, 2, TILE), np.float32)
    leave = np.zeros((2, TILE, 2, TILE), np.float32)
    for half in range(2):
        enter[half, half, :, 0] = enter[half, half, :, 1] = move
        leave[half, :, half] = move.T
    rows = np.concatenate([enter.reshape(4 * TILE, -1), leave.reshape(2 * TILE, -1)])
    return tiles.reshape(4 * TILE, 4 * TILE), rows.reshape(3, 2 * TILE, 2 * TILE)


STEPS = chebyshev_steps(3)
COARSE_STEPS = chebyshev_steps(8)


def halves(u):
    high = u.astype(BF16).astype(F32)
    return jnp.concatenate([high, u - high], 0).astype(BF16)


def twice(out):
    total = out[:LOADS] + out[LOADS:]
    return jnp.concatenate([total, total], 1)


def apply_one(u, tile):
    return twice(
        lax.dot_general(halves(u), tile, (((1,), (1,)), ((), ())), preferred_element_type=F32)
    )


def apply_two(u, w, tiles):
    left = jnp.concatenate([halves(u), halves(w)], 1)
    return twice(
        lax.dot_general(left, tiles, (((1,), (1,)), ((), ())), preferred_element_type=F32)
    )


def apply_transposed(u, tile):
    out = lax.dot_general(
        halves(u)[:, :TILE], tile, (((1,), (0,)), ((), ())), preferred_element_type=F32
    )
    total = out[:LOADS] + out[LOADS:]
    return total + pltpu.roll(total, TILE, 1)


def rows_loop(count, compute, store, unroll=UNROLL):
    def step(turn, carry):
        base = turn * unroll
        results = [compute(base + j) for j in range(unroll)]
        for j in range(unroll):
            store(base + j, results[j])
        return carry

    lax.fori_loop(0, count // unroll, step, 0)


def exact_dot(value, matrix):
    high = value.astype(BF16)
    rest = value - high.astype(F32)
    middle = rest.astype(BF16)
    small = (rest - middle.astype(F32)).astype(BF16)
    first, second, third = (
        jnp.dot(part, matrix, preferred_element_type=F32) for part in (high, middle, small)
    )
    return first + second + third


def converted(tiles, matrix):
    value = jnp.concatenate(tiles, 0)
    high = value.astype(BF16)
    small = (value - high.astype(F32)).astype(BF16)
    both = jnp.concatenate([high, small], 1)
    return jnp.dot(both, matrix, preferred_element_type=F32).astype(BF16)


def keep_tile(ref, i, lanes, rows):
    ref[i, : TILE // 2, lanes] = rows[:, : 2 * TILE]
    ref[i, TILE // 2 :, lanes] = rows[:, 2 * TILE :]


def convert_single(raw, ref, matrix, count):
    def step(turn, carry):
        base = pl.multiple_of(turn * GROUP * TILE // 2, GROUP * TILE // 2)
        tiles = [raw[pl.ds(base + j, TILE // 2, stride=GROUP), :] for j in range(GROUP)]
        out = converted(tiles, matrix[...])
        for j in range(GROUP):
            rows = out[j * TILE // 2 : (j + 1) * TILE // 2]
            keep_tile(ref, turn * GROUP + j, slice(0, 2 * TILE), rows)
        return carry

    lax.fori_loop(0, count // GROUP, step, 0)


def convert_double(raw, ref, matrix, count):
    def step(turn, carry):
        base = pl.multiple_of(turn * GROUP * TILE // 2, GROUP * TILE // 2)
        tiles = [
            raw[pl.ds(base + j * TILE + k, TILE // 2, stride=2), :]
            for j in range(GROUP // 2)
            for k in range(2)
        ]
        out = converted(tiles, matrix[...])
        for j in range(GROUP // 2):
            for k in range(2):
                place = 2 * j + k
                rows = out[place * TILE // 2 : (place + 1) * TILE // 2]
                lanes = slice(2 * TILE * k, 2 * TILE * (k + 1))
                keep_tile(ref, turn * (GROUP // 2) + j, lanes, rows)
        return carry

    lax.fori_loop(0, count // (GROUP // 2), step, 0)


def kernel(
    groups,
    size,
    matrix,
    moves,
    rhs_in,
    ghost_rows,
    cols_one,
    diag_one_raw,
    offd_one_raw,
    prol_one_raw,
    agg_one,
    hot_one,
    cols_two,
    cols_two_in,
    diag_two_raw,
    offd_two_raw,
    prol_two_raw,
    agg_two,
    hot_two,
    cols_three,
    diag_three_raw,
    offd_three_raw,
    out_ref,
    coarse_out,
    *scratch,
):
    raws = (
        diag_one_raw,
        offd_one_raw,
        prol_one_raw,
        diag_two_raw,
        offd_two_raw,
        prol_two_raw,
        diag_three_raw,
        offd_three_raw,
    )
    staged, tiles, scratch = scratch[:8], scratch[8:16], scratch[16:]
    diag_one, offd_one, prol_one, diag_two, offd_two, prol_two, diag_three, offd_three = tiles
    (
        rhs_one,
        win_one,
        send_one,
        got_one,
        x_one,
        r_one,
        win_two,
        send_two,
        got_two,
        x_two,
        r_two,
        rhs_two,
        terms,
        part,
        half_in,
        pair_send,
        pair_in,
        pair_all,
        terms_two,
        coarse_part,
        gather_a,
        gather_b,
        packed_c,
        full_c,
        d_three,
        r_three,
        coarse_ref,
        lists_in,
        lists,
        cols_in,
        cols_near,
        stage_sem,
        list_sem,
        send_sem_one,
        recv_sem_one,
        send_sem_two,
        recv_sem_two,
        half_sem,
        pair_sem,
        sem_a,
        sem_b,
        sem_c,
    ) = scratch
    stages = [
        pltpu.make_async_copy(raws[k], staged[k], stage_sem.at[k]) for k in range(8)
    ]
    for stage in stages:
        stage.start()

    def prepare(k, convert, count):
        stages[k].wait()
        convert(staged[k], tiles[k], matrix, count)

    g, e = lax.axis_index("grp"), lax.axis_index("dev")
    me = g * size + e
    last = groups * size - 1
    pair, h = me // 2, me % 2
    pairs = groups * size // 2
    own = HALF + HALF * h
    has_left, has_right = me > 0, me < last
    has_prev, has_next = pair > 0, pair < pairs - 1
    share = COARSE // size

    def at(index):
        return (index // size, index % size)

    lanes = lax.broadcasted_iota(jnp.int32, (LOADS, 2 * TILE), 1)
    low = lanes < TILE

    def unpack(packed):
        turned = pltpu.roll(packed, TILE, 1)
        return jnp.where(low, packed, turned), jnp.where(low, turned, packed)

    barrier = pltpu.get_barrier_semaphore()

    def greet(device):
        pl.semaphore_signal(barrier, inc=1, device_id=device, device_id_type=MESH)

    for k in range(1, size):
        greet((g, (e + k) % size))
    for k in range(1, groups):
        greet(((g + k) % groups, e))

    @pl.when(has_left)
    def _():
        greet(at(me - 1))

    @pl.when(has_right)
    def _():
        greet(at(me + 1))

    @pl.when(has_prev)
    def _():
        greet(at(me - 2))

    @pl.when(has_next)
    def _():
        greet(at(me + 2))

    for q in range(LOADS // 2):
        value = rhs_in[:, 2 * TILE * q : 2 * TILE * (q + 1)]
        for half in range(2):
            rhs_one[pl.ds(2 * q + half, ROWS, stride=LOADS), :] = exact_dot(value, moves[half])

    prepare(0, convert_single, ROWS)

    def one(flag):
        return flag.astype(jnp.int32)

    expected = size - 1 + groups - 1 + one(has_left) + one(has_right)
    pl.semaphore_wait(barrier, expected + one(has_prev) + one(has_next))

    def list_copy(kind, side):
        step = kind + 1
        return pltpu.make_async_remote_copy(
            src_ref=(ghost_rows, cols_two_in)[kind],
            dst_ref=(lists_in, cols_in)[kind].at[1 - side],
            send_sem=list_sem.at[0, kind, side],
            recv_sem=list_sem.at[1, kind, 1 - side],
            device_id=at(me - step) if side == 0 else at(me + step),
            device_id_type=MESH,
        )

    neighbours = ((has_left, has_right), (has_prev, has_next))
    for kind in range(2):
        for side in range(2):

            @pl.when(neighbours[kind][side])
            def _(kind=kind, side=side):
                list_copy(kind, side).start()

    prepare(1, convert_double, ROWS)

    def take_lists(kind):
        for side in range(2):

            @pl.when(neighbours[kind][side])
            def _(side=side):
                list_copy(kind, 1 - side).wait_recv()
                list_copy(kind, side).wait_send()
                local = pltpu.make_async_copy(
                    (lists_in, cols_in)[kind].at[side],
                    (lists, cols_near)[kind].at[side],
                    list_sem.at[2, kind, side],
                )
                local.start()
                local.wait()

    take_lists(0)
    take_lists(1)

    def rhs_row(i):
        return rhs_one[pl.ds(pl.multiple_of(i * LOADS, LOADS), LOADS), :]

    def level_one(s, store, during=None):
        def copy(side):
            target = at(me - 1) if side == 0 else at(me + 1)
            return pltpu.make_async_remote_copy(
                src_ref=send_one.at[s, side],
                dst_ref=got_one.at[s, 1 - side],
                send_sem=send_sem_one.at[s, side],
                recv_sem=recv_sem_one.at[s, 1 - side],
                device_id=target,
                device_id_type=MESH,
            )

        flags = (has_left, has_right)
        for side in range(2):

            @pl.when(flags[side])
            def _(side=side):
                for t in range(GHOST // 2):
                    first = win_one[s, GHOST + lists[side, 1 - side, t]]
                    second = win_one[s, GHOST + lists[side, 1 - side, t + GHOST // 2]]
                    send_one[s, side, t] = jnp.where(low, first, second)
                copy(side).start()

        def diag(i):
            return r_one[i] - apply_one(win_one[s, GHOST + i], diag_one[i])

        def keep(i, value):
            r_one[i] = value

        rows_loop(ROWS, diag, keep)
        if during:
            during()
        for side in range(2):
            base = 0 if side == 0 else GHOST + ROWS

            @pl.when(flags[side])
            def _(side=side, base=base):
                copy(1 - side).wait_recv()
                copy(side).wait_send()
                for t in range(GHOST // 2):
                    first, second = unpack(got_one[s, side, t])
                    win_one[s, base + t] = first
                    win_one[s, base + t + GHOST // 2] = second

            @pl.when(jnp.logical_not(flags[side]))
            def _(base=base):
                win_one[s, base : base + GHOST] = jnp.zeros((GHOST, LOADS, 2 * TILE), F32)

        def offd(i):
            return r_one[i] - apply_two(
                win_one[s, cols_one[0, i]], win_one[s, cols_one[1, i]], offd_one[i]
            )

        rows_loop(ROWS, offd, store)

    def level_two(s, store, during=None):
        def partner_copy():
            return pltpu.make_async_remote_copy(
                src_ref=send_two.at[s, 2],
                dst_ref=got_two.at[s, 2],
                send_sem=send_sem_two.at[s, 2],
                recv_sem=recv_sem_two.at[s, 2],
                device_id=at(me + 1 - 2 * h),
                device_id_type=MESH,
            )

        def pair_copy(side):
            return pltpu.make_async_remote_copy(
                src_ref=send_two.at[s, side],
                dst_ref=got_two.at[s, 1 - side],
                send_sem=send_sem_two.at[s, side],
                recv_sem=recv_sem_two.at[s, 1 - side],
                device_id=at(me - 2) if side == 0 else at(me + 2),
                device_id_type=MESH,
            )

        def take(slot, base):
            for t in range(HALF // 2):
                first, second = unpack(got_two[s, slot, t])
                win_two[s, base + t] = first
                win_two[s, base + t + HALF // 2] = second

        for t in range(HALF // 2):
            send_two[s, 2, t] = jnp.where(
                low, win_two[s, own + t], win_two[s, own + t + HALF // 2]
            )
        partner_copy().start()

        def diag(first):
            def compute(j):
                return r_two[first + j] - apply_one(
                    win_two[s, own + first + j], diag_two[first + j]
                )

            def keep(j, value):
                r_two[first + j] = value

            rows_loop(HALF // 2, compute, keep)

        diag(0)
        partner_copy().wait()
        take(2, HALF + HALF * (1 - h))
        flags = (has_prev, has_next)

        def wanted(side, t):
            if side == 0:
                row = jnp.maximum(cols_near[0, 1, t] - 2 * ROWS, 0)
            else:
                row = jnp.minimum(cols_near[1, 0, t], ROWS - 1)
            return win_two[s, HALF + row]

        for side in range(2):

            @pl.when(flags[side])
            def _(side=side):
                for t in range(HALF // 2):
                    send_two[s, side, t] = jnp.where(
                        low, wanted(side, t), wanted(side, t + HALF // 2)
                    )
                pair_copy(side).start()

        diag(HALF // 2)
        if during:
            during()
        for side in range(2):
            base = 0 if side == 0 else HALF + ROWS

            @pl.when(flags[side])
            def _(side=side, base=base):
                pair_copy(1 - side).wait_recv()
                pair_copy(side).wait_send()
                take(side, base)

            @pl.when(jnp.logical_not(flags[side]))
            def _(base=base):
                win_two[s, base : base + HALF] = jnp.zeros((HALF, LOADS, 2 * TILE), F32)

        def offd(j):
            before, after = cols_two[0, j], cols_two[1, j]
            before = jnp.where(before < ROWS, j, before - HALF)
            after = jnp.where(
                after < 2 * ROWS, jnp.maximum(after, ROWS) - HALF, HALF + ROWS + j
            )
            return r_two[j] - apply_two(win_two[s, before], win_two[s, after], offd_two[j])

        rows_loop(HALF, offd, store)

    for i in range(ROWS):
        value = rhs_row(i)
        r_one[i] = value
        win_one[0, GHOST + i] = value / CENTER
        x_one[i] = value / CENTER

    def smooth_one(s, step, during=None):
        old, new = STEPS[step]

        def store(i, value):
            r_one[i] = value
            turn = old * win_one[s, GHOST + i] + new * value
            win_one[s + 1, GHOST + i] = turn
            x_one[i] = x_one[i] + turn

        level_one(s, store, during)

    def keep_one(i, value):
        r_one[i] = value

    smooth_one(0, 0, lambda: prepare(2, convert_single, ROWS))
    smooth_one(1, 1, lambda: prepare(3, convert_single, HALF))
    level_one(2, keep_one, lambda: prepare(4, convert_double, HALF))

    def restrict_one(i, value):
        terms[pl.ds(pl.multiple_of(i * LOADS, LOADS), LOADS), :] = value

    rows_loop(ROWS, lambda i: apply_transposed(r_one[i], prol_one[i]), restrict_one)

    def gathered(hot_ref, terms_ref, part_ref, count, fine):
        row = lax.broadcasted_iota(jnp.int32, (count, fine), 0)
        hot = jnp.where(row == hot_ref[...], 1.0, 0.0).astype(BF16)
        wide = lax.broadcasted_iota(jnp.int32, (fine, 2 * TILE), 1) < TILE
        for v in range(LOADS):
            value = terms_ref[pl.ds(v, fine, stride=LOADS), :]
            high = value.astype(BF16).astype(F32)
            mixed = jnp.where(wide, high, value - high).astype(BF16)
            out = jnp.dot(hot, mixed, preferred_element_type=F32)
            part_ref[pl.ds(v, count, stride=LOADS), :] = out + pltpu.roll(out, TILE, 1)

    gathered(hot_one, terms, part, ROWS, ROWS)

    partner = at(me + 1 - 2 * h)
    mine, theirs = HALF * LOADS * h, HALF * LOADS * (1 - h)

    def part_rows(base, j):
        return part[pl.ds(pl.multiple_of(base + j * LOADS, LOADS), LOADS), :]

    for t in range(HALF // 2):
        pair_send[0, t] = jnp.where(
            low, part_rows(theirs, t), part_rows(theirs, t + HALF // 2)
        )
    half_copy = pltpu.make_async_remote_copy(
        src_ref=pair_send.at[0],
        dst_ref=half_in,
        send_sem=half_sem.at[0],
        recv_sem=half_sem.at[1],
        device_id=partner,
        device_id_type=MESH,
    )
    half_copy.start()
    half_copy.wait()
    for t in range(HALF // 2):
        for j, other in zip((t, t + HALF // 2), unpack(half_in[t])):
            value = part_rows(mine, j) + other
            rhs_two[j] = value
            r_two[j] = value
            win_two[0, own + j] = value / CENTER
            x_two[j] = value / CENTER

    def smooth_two(s, step, during=None):
        old, new = STEPS[step]

        def store(j, value):
            r_two[j] = value
            turn = old * win_two[s, own + j] + new * value
            x_two[j] = x_two[j] + turn
            win_two[s + 1, own + j] = turn

        level_two(s, store, during)

    def keep_two(j, value):
        r_two[j] = value

    smooth_two(0, 0, lambda: prepare(5, convert_single, HALF))
    smooth_two(1, 1, lambda: prepare(6, convert_single, COARSE))
    level_two(2, keep_two, lambda: prepare(7, convert_double, COARSE))

    def restrict_two(j, value):
        terms_two[pl.ds(pl.multiple_of(j * LOADS, LOADS), LOADS), :] = value

    rows_loop(HALF, lambda j: apply_transposed(r_two[j], prol_two[j]), restrict_two)
    gathered(hot_two, terms_two, coarse_part, COARSE, HALF)

    fold = 2 - share % 2
    unit = share // fold

    for c in range(size * unit):
        member, r = c // unit, c % unit
        first = (member * share + r) * LOADS
        value = coarse_part[first : first + LOADS, :]
        if fold == 2:
            second = first + unit * LOADS
            value = jnp.where(low, value, coarse_part[second : second + LOADS, :])
        packed_c[member, r * LOADS : (r + 1) * LOADS] = value

    def copy_a(k):
        target = (e + k) % size
        return pltpu.make_async_remote_copy(
            src_ref=packed_c.at[target],
            dst_ref=gather_a.at[k],
            send_sem=sem_a.at[0, k],
            recv_sem=sem_a.at[1, k],
            device_id=(g, target),
            device_id_type=MESH,
        )

    for k in range(1, size):
        copy_a(k).start()
    total = packed_c[e]
    for k in range(1, size):
        copy_a(k).wait()
        total = total + gather_a[k]
    gather_b[g] = total

    def copy_b(k, member):
        return pltpu.make_async_remote_copy(
            src_ref=gather_b.at[g],
            dst_ref=gather_b.at[member],
            send_sem=sem_b.at[0, k],
            recv_sem=sem_b.at[1, k],
            device_id=((g + k) % groups, e),
            device_id_type=MESH,
        )

    for k in range(1, groups):
        copy_b(k, g).start()
    for k in range(1, groups):
        copy_b(k, g).wait_send()
        copy_b(k, (g + groups - k) % groups).wait_recv()
    total = gather_b[0]
    for k in range(1, groups):
        total = total + gather_b[k]
    full_c[e] = total

    def copy_c(k, member):
        return pltpu.make_async_remote_copy(
            src_ref=full_c.at[e],
            dst_ref=full_c.at[member],
            send_sem=sem_c.at[0, k],
            recv_sem=sem_c.at[1, k],
            device_id=(g, (e + k) % size),
            device_id_type=MESH,
        )

    for k in range(1, size):
        copy_c(k, e).start()
    for k in range(1, size):
        copy_c(k, e).wait_send()
        copy_c(k, (e + size - k) % size).wait_recv()

    for c in range(size * unit):
        member, r = c // unit, c % unit
        value = full_c[member, r * LOADS : (r + 1) * LOADS]
        values = unpack(value) if fold == 2 else (value,)
        for k, value in enumerate(values):
            row = member * share + r + k * unit
            r_three[row] = value
            d_three[0, row] = value / CENTER
            coarse_ref[row] = value / CENTER

    for s, (old, new) in enumerate(COARSE_STEPS):
        now, later = s % 2, 1 - s % 2

        def coarse(c, now=now):
            return (
                r_three[c]
                - apply_one(d_three[now, c], diag_three[c])
                - apply_two(
                    d_three[now, cols_three[0, c]],
                    d_three[now, cols_three[1, c]],
                    offd_three[c],
                )
            )

        def store(c, value, now=now, later=later, old=old, new=new):
            r_three[c] = value
            turn = old * d_three[now, c] + new * value
            d_three[later, c] = turn
            coarse_ref[c] = coarse_ref[c] + turn

        rows_loop(COARSE, coarse, store, 16)

    def corrected_two(j):
        return x_two[j] + apply_one(coarse_ref[agg_two[j]], prol_two[j])

    def store_two(j, value):
        x_two[j] = value
        r_two[j] = rhs_two[j]
        win_two[3, own + j] = value

    rows_loop(HALF, corrected_two, store_two)

    def first_two(j, value):
        r_two[j] = value
        turn = value / CENTER
        win_two[4, own + j] = turn
        x_two[j] = x_two[j] + turn

    level_two(3, first_two)
    smooth_two(4, 0)

    def last_two(j, value):
        turn = STEPS[1][0] * win_two[5, own + j] + STEPS[1][1] * value
        pair_all[HALF * h + j] = x_two[j] + turn

    level_two(5, last_two)
    for t in range(HALF // 2):
        pair_send[1, t] = jnp.where(
            low, pair_all[HALF * h + t], pair_all[HALF * h + t + HALF // 2]
        )
    pair_copy = pltpu.make_async_remote_copy(
        src_ref=pair_send.at[1],
        dst_ref=pair_in,
        send_sem=pair_sem.at[0],
        recv_sem=pair_sem.at[1],
        device_id=partner,
        device_id_type=MESH,
    )
    pair_copy.start()
    pair_copy.wait()
    for t in range(HALF // 2):
        first, second = unpack(pair_in[t])
        pair_all[HALF * (1 - h) + t] = first
        pair_all[HALF * (1 - h) + t + HALF // 2] = second

    def corrected_one(i):
        return x_one[i] + apply_one(pair_all[agg_one[i]], prol_one[i])

    def store_one(i, value):
        x_one[i] = value
        r_one[i] = rhs_row(i)
        win_one[3, GHOST + i] = value

    rows_loop(ROWS, corrected_one, store_one)

    def first_one(i, value):
        r_one[i] = value
        turn = value / CENTER
        win_one[4, GHOST + i] = turn
        x_one[i] = x_one[i] + turn

    level_one(3, first_one)
    smooth_one(4, 0)

    def last_one(i, value):
        turn = STEPS[1][0] * win_one[5, GHOST + i] + STEPS[1][1] * value
        terms[pl.ds(pl.multiple_of(i * LOADS, LOADS), LOADS), :] = x_one[i] + turn

    level_one(5, last_one)

    def leave(stage_ref, target_ref, count):
        wide = lax.broadcasted_iota(jnp.int32, (count, 2 * TILE), 1) < TILE
        for q in range(LOADS // 2):
            first = stage_ref[pl.ds(2 * q, count, stride=LOADS), :]
            second = stage_ref[pl.ds(2 * q + 1, count, stride=LOADS), :]
            target_ref[:, 2 * TILE * q : 2 * TILE * (q + 1)] = exact_dot(
                jnp.where(wide, first, second), moves[2]
            )

    leave(terms, out_ref, ROWS)
    for c in range(COARSE):
        coarse_part[c * LOADS : (c + 1) * LOADS, :] = coarse_ref[c]
    leave(coarse_part, coarse_out, COARSE)


def single(flat):
    count = flat.shape[0]
    tiles = flat.reshape(count // GROUP, GROUP, TILE // 2, 2 * TILE)
    return tiles.transpose(0, 2, 1, 3).reshape(count * TILE // 2, 2 * TILE)


def double(flat):
    count = flat.shape[0]
    tiles = flat.reshape(count, 2, TILE // 2, 2 * TILE)
    return tiles.transpose(0, 2, 1, 3).reshape(count * TILE, 2 * TILE)


def body(
    groups,
    size,
    right_side,
    ghost_rows,
    cols_one,
    diag_one,
    offd_one,
    prol_one,
    agg_one,
    cols_two,
    diag_two,
    offd_two,
    prol_two,
    agg_two,
    cols_three,
    diag_three,
    offd_three,
):
    matrix, moves = (jnp.asarray(a, BF16) for a in spread())
    smem = pl.BlockSpec(memory_space=pltpu.SMEM)
    vmem = pl.BlockSpec(memory_space=pltpu.VMEM)
    row = (LOADS, 2 * TILE)
    share = COARSE // size
    unit = share // (2 - share % 2) * LOADS
    dma = pltpu.SemaphoreType.DMA
    hbm = pl.BlockSpec(memory_space=pl.ANY)
    raw = [
        single(diag_one),
        double(offd_one),
        single(prol_one),
        single(diag_two),
        double(offd_two),
        single(prol_two),
        single(diag_three),
        double(offd_three),
    ]
    widths = [2, 4, 2, 2, 4, 2, 2, 4]
    counts = [ROWS] * 3 + [HALF] * 3 + [COARSE] * 2
    return pl.pallas_call(
        functools.partial(kernel, groups, size),
        out_shape=(
            jax.ShapeDtypeStruct((ROWS, LOADS * TILE), F32),
            jax.ShapeDtypeStruct((COARSE, LOADS * TILE), F32),
        ),
        in_specs=[vmem] * 4
        + [smem, hbm, hbm, hbm, smem, vmem]
        + [smem, vmem, hbm, hbm, hbm, smem, vmem]
        + [smem, hbm, hbm],
        out_specs=(vmem, vmem),
        scratch_shapes=[pltpu.VMEM(a.shape, F32) for a in raw]
        + [pltpu.VMEM((n, TILE, w * TILE), BF16) for n, w in zip(counts, widths)]
        + [
            pltpu.VMEM((ROWS * LOADS, 2 * TILE), F32),
            pltpu.VMEM((6, ROWS + 2 * GHOST, *row), F32),
            pltpu.VMEM((6, 2, GHOST // 2, *row), F32),
            pltpu.VMEM((6, 2, GHOST // 2, *row), F32),
            pltpu.VMEM((ROWS, *row), F32),
            pltpu.VMEM((ROWS, *row), F32),
            pltpu.VMEM((6, ROWS + 2 * HALF, *row), F32),
            pltpu.VMEM((6, 3, HALF // 2, *row), F32),
            pltpu.VMEM((6, 3, HALF // 2, *row), F32),
            pltpu.VMEM((HALF, *row), F32),
            pltpu.VMEM((HALF, *row), F32),
            pltpu.VMEM((HALF, *row), F32),
            pltpu.VMEM((ROWS * LOADS, 2 * TILE), F32),
            pltpu.VMEM((ROWS * LOADS, 2 * TILE), F32),
            pltpu.VMEM((HALF // 2, *row), F32),
            pltpu.VMEM((2, HALF // 2, *row), F32),
            pltpu.VMEM((HALF // 2, *row), F32),
            pltpu.VMEM((ROWS, *row), F32),
            pltpu.VMEM((HALF * LOADS, 2 * TILE), F32),
            pltpu.VMEM((COARSE * LOADS, 2 * TILE), F32),
            pltpu.VMEM((size, unit, 2 * TILE), F32),
            pltpu.VMEM((groups, unit, 2 * TILE), F32),
            pltpu.VMEM((size, unit, 2 * TILE), F32),
            pltpu.VMEM((size, unit, 2 * TILE), F32),
            pltpu.VMEM((2, COARSE, *row), F32),
            pltpu.VMEM((COARSE, *row), F32),
            pltpu.VMEM((COARSE, *row), F32),
            pltpu.VMEM((2, 2, GHOST), jnp.int32),
            pltpu.SMEM((2, 2, GHOST), jnp.int32),
            pltpu.VMEM((2, 2, HALF), jnp.int32),
            pltpu.SMEM((2, 2, HALF), jnp.int32),
            dma((8,)),
            dma((3, 2, 2)),
            dma((6, 2)),
            dma((6, 2)),
            dma((6, 3)),
            dma((6, 3)),
            dma((2,)),
            dma((2,)),
            dma((2, size)),
            dma((2, groups)),
            dma((2, size)),
        ],
        compiler_params=pltpu.CompilerParams(
            collective_id=0, has_side_effects=True, vmem_limit_bytes=56 * 2**20
        ),
    )(
        matrix,
        moves,
        right_side,
        ghost_rows,
        cols_one.T,
        *raw[:3],
        agg_one,
        agg_one[None],
        cols_two.T,
        cols_two.T,
        *raw[3:6],
        agg_two,
        agg_two[None],
        cols_three.T,
        *raw[6:],
    )


def solution(mesh):
    groups, size = mesh.shape["grp"], mesh.shape["dev"]
    rows = P(("grp", "dev"), None)
    tiles = P(("grp", "dev"), None, None)
    flat = P(("grp", "dev"))
    return jax.shard_map(
        functools.partial(body, groups, size),
        mesh=mesh,
        in_specs=(
            rows,
            rows,
            rows,
            rows,
            tiles,
            rows,
            flat,
            rows,
            rows,
            tiles,
            rows,
            flat,
            P(),
            P(),
            P(),
        ),
        out_specs=(rows, P()),
        check_vma=False,
    )
```
